32 devices in a mesh: grp: 2 (over y), gx: 4 (over z), gy: 2 (over x), gz: 2 (over core).
Axes of the slice: x: 2, y: 2, z: 4, core: 2. Of those that a mesh axis runs over, the one named last changes fastest.
Arguments:
- fine_latent: bfloat16 [32768, 128], P(('grp', 'gx', 'gy', 'gz')), parts along dimension 0, may hold values from -6 to 6
- fine_edges: bfloat16 [131072, 128], P(('grp', 'gx', 'gy', 'gz')), parts along dimension 0, may hold values from -6 to 6
- fine_from: int32 [131072], P(('grp', 'gx', 'gy', 'gz')), parts along dimension 0, may hold values from 0 to 1535, as said below
- fine_to: int32 [131072], P(('grp', 'gx', 'gy', 'gz')), parts along dimension 0, may hold values from 0 to 1023
- fine_send_x: int32 [64, 128], P(('grp', 'gx', 'gy', 'gz')), parts along dimension 0, may hold values from 0 to 1023
- fine_send_yz: int32 [128, 64], P(('grp', 'gx', 'gy', 'gz')), parts along dimension 0, may hold values from 0 to 1023
- cluster: int32 [32768], P(('grp', 'gx', 'gy', 'gz')), parts along dimension 0, may hold values from 0 to 127, as said below
- coarse_edges: bfloat16 [16384, 128], P(('grp', 'gx', 'gy', 'gz')), parts along dimension 0, may hold values from -6 to 6
- coarse_from: int32 [16384], P(('grp', 'gx', 'gy', 'gz')), parts along dimension 0, may hold values from 0 to 191, as said below
- coarse_to: int32 [16384], P(('grp', 'gx', 'gy', 'gz')), parts along dimension 0, may hold values from 0 to 127
- coarse_send_x: int32 [64, 16], P(('grp', 'gx', 'gy', 'gz')), parts along dimension 0, may hold values from 0 to 127
- coarse_send_yz: int32 [128, 8], P(('grp', 'gx', 'gy', 'gz')), parts along dimension 0, may hold values from 0 to 127
- edge_in: bfloat16 [2, 384, 128], replicated, may hold values from -0.3125 to 0.3125
- edge_out: bfloat16 [2, 128, 128], replicated, may hold values from -0.5 to 0.5
- node_in: bfloat16 [2, 256, 128], replicated, may hold values from -0.375 to 0.375
- node_out: bfloat16 [2, 128, 128], replicated, may hold values from -0.5 to 0.5
- norm_gain: float32 [2, 2, 128], replicated, may hold values from 0.1 to 1.9
- unpool_weight: bfloat16 [128, 128], replicated, may hold values from -0.5 to 0.5
Outputs:
- fine_out: bfloat16 [32768, 128], P(('grp', 'gx', 'gy', 'gz')), parts along dimension 0
The draws below stay inside these ranges and needn't reach their ends.
There are 2 independent parts, one for each index of `grp`. The reference program is written for one: setup_inputs(seed, part) draws one part's arguments, and reference() takes and returns one part's arrays. A program takes and returns all parts, laid end to end along the dimension named above; an argument that names none is the same for every part. Nothing has to cross between parts.
Inputs may be any that keep to these rules, and one draw needn't show every extreme that they name: `cluster`: each of the 128 coarse nodes of a box is named by at least one fine node of that box. `fine_from`: rows below 1024 are the box's own; about a fifth of the edges read a received row. `coarse_from`: rows below 128 are the box's own; about a fifth of the edges read a received row.
All inputs are finite; a program needn't handle non-finite values.
Results may differ from the reference program's by a relative error of at most 0.0064.
Values may be sent and summed in bfloat16 or wider, within the bound.
No kernel may reach another device: no remote copies, remote signals or barrier semaphores. Data moves between devices by JAX's collectives and lax.ppermute only.
A program may use at most 64 MiB of HBM per device.

```python
import jax
import jax.numpy as jnp
from jax import lax

D = 128
NF = 1024
BOXES = 16
EF = 4096
HX = 128
HY = 64
NC = 128
EC = 512
CHX = 16
CHY = 8
N_GX = 4
N_GY = 2
N_GZ = 2


def draw_cluster(key, part):
    key = jax.random.fold_in(key, 7)
    box_keys = jax.random.split(key, BOXES)

    def one_box(box_key):
        first_key, second_key = jax.random.split(box_key)
        order = jax.random.permutation(first_key, NF)
        labels = jax.random.randint(second_key, (NF,), 0, NC, dtype=jnp.int32)
        return labels.at[order[:NC]].set(jnp.arange(NC, dtype=jnp.int32))
    return jax.vmap(one_box)(box_keys).reshape(-1).astype(jnp.int32)


def sender_rows(key, count, own_rows, halo_rows):
    pick_key, own_key, halo_key = jax.random.split(key, 3)
    pick = jax.random.randint(pick_key, (count,), 0, 5, dtype=jnp.int32)
    own_pick = jax.random.randint(own_key, (count,), 0, own_rows, dtype=jnp.int32)
    halo_pick = own_rows + jax.random.randint(halo_key, (count,), 0, halo_rows, dtype=jnp.int32)
    return jnp.where(pick == 0, halo_pick, own_pick).astype(jnp.int32)


def draw_fine_from(key, part):
    key = jax.random.fold_in(key, 11)
    return sender_rows(key, BOXES * EF, NF, 2 * HX + 4 * HY)


def draw_coarse_from(key, part):
    key = jax.random.fold_in(key, 13)
    return sender_rows(key, BOXES * EC, NC, 2 * CHX + 4 * CHY)


def place_ends(drawn, rng, least, top_value):
    longest = drawn.shape.index(max(drawn.shape))
    spots = []
    for shift in (0, 1):
        where = [jax.random.randint(jax.random.fold_in(rng, axis), (), 0, length) for axis, length in enumerate(drawn.shape)]
        where[longest] = (where[longest] + shift) % drawn.shape[longest]
        spots.append(tuple(where))
    return drawn.at[spots[0]].set(least).at[spots[1]].set(top_value)


def block_levels(key, shape, shards, smallest, high):
    loudness, own = 1.0, jax.random.fold_in(key, 6)
    for position, parts in shards:
        draws = jnp.exp(jax.random.uniform(jax.random.fold_in(own, position), (parts,), jnp.float32, smallest / len(shards), high / len(shards)))
        loudness = loudness * jnp.repeat(draws, shape[position] // parts).reshape([-1 if axis == position else 1 for axis in range(len(shape))])
    return loudness


def bell_draw(stream_key, shape, width, reach, cuts=(), held_as=jnp.bfloat16):
    entries = jax.random.normal(stream_key, shape, jnp.float32) * width
    if len(cuts) > 0:
        entries = block_levels(stream_key, shape, cuts, -0.22, 0.18) * entries
    return jnp.clip(entries, min=-reach, max=reach).astype(held_as)


def setup_inputs(seed: int = 0, part: int = 0) -> dict:
    splits = jax.random.split(jax.random.key(seed), 19)
    own_keys = jax.random.split(jax.random.fold_in(splits[18], part), 19)
    return {
        "fine_latent": bell_draw(own_keys[0], (BOXES * NF, D), 1.0, 6.0, ((0, 16),)),
        "fine_edges": bell_draw(own_keys[1], (BOXES * EF, D), 1.0, 6.0, ((0, 16),)),
        "fine_from": draw_fine_from(jax.random.fold_in(jax.random.fold_in(splits[18], part), 71), part),
        "fine_to": place_ends(jax.random.randint(own_keys[3], (BOXES * EF,), 0, NF), jax.random.fold_in(own_keys[3], 1), 0, NF - 1).astype(jnp.int32),
        "fine_send_x": place_ends(jax.random.randint(own_keys[4], (2 * BOXES, HX), 0, NF), jax.random.fold_in(own_keys[4], 1), 0, NF - 1).astype(jnp.int32),
        "fine_send_yz": place_ends(jax.random.randint(own_keys[5], (4 * BOXES, HY), 0, NF), jax.random.fold_in(own_keys[5], 1), 0, NF - 1).astype(jnp.int32),
        "cluster": draw_cluster(jax.random.fold_in(jax.random.fold_in(splits[18], part), 71), part),
        "coarse_edges": bell_draw(own_keys[7], (BOXES * EC, D), 1.0, 6.0, ((0, 16),)),
        "coarse_from": draw_coarse_from(jax.random.fold_in(jax.random.fold_in(splits[18], part), 71), part),
        "coarse_to": place_ends(jax.random.randint(own_keys[9], (BOXES * EC,), 0, NC), jax.random.fold_in(own_keys[9], 1), 0, NC - 1).astype(jnp.int32),
        "coarse_send_x": place_ends(jax.random.randint(own_keys[10], (2 * BOXES, CHX), 0, NC), jax.random.fold_in(own_keys[10], 1), 0, NC - 1).astype(jnp.int32),
        "coarse_send_yz": place_ends(jax.random.randint(own_keys[11], (4 * BOXES, CHY), 0, NC), jax.random.fold_in(own_keys[11], 1), 0, NC - 1).astype(jnp.int32),
        "edge_in": bell_draw(splits[12], (2, 3 * D, D), (3 * D) ** -0.5, 0.3125),
        "edge_out": bell_draw(splits[13], (2, D, D), D ** -0.5, 0.5),
        "node_in": bell_draw(splits[14], (2, 2 * D, D), (2 * D) ** -0.5, 0.375),
        "node_out": bell_draw(splits[15], (2, D, D), D ** -0.5, 0.5),
        "norm_gain": jnp.clip(1.0 + 0.18 * jax.random.normal(splits[16], (2, 2, D), jnp.float32), 0.1, 1.9),
        "unpool_weight": bell_draw(splits[17], (D, D), D ** -0.5, 0.5),
    }


EPSILON = 1e-05

def layer_norm(values, scales):
    centre = lax.optimization_barrier(jnp.mean(values, axis=-1, keepdims=True))
    centred = values - centre
    spread = lax.optimization_barrier(jnp.mean(centred * centred, axis=-1, keepdims=True))
    return centred * lax.rsqrt(spread + EPSILON) * scales.astype(jnp.float32)

def two_layer(inputs, first_w, second_w, scales):
    hidden = jnp.maximum(jnp.dot(inputs, first_w, preferred_element_type=jnp.float32), 0.0).astype(jnp.bfloat16)
    return layer_norm(jnp.dot(hidden, second_w, preferred_element_type=jnp.float32), scales)

def from_lower(values, axis_id):
    length_along = values.shape[axis_id]
    kept_part = lax.slice_in_dim(values, 0, length_along - 1, axis=axis_id)
    empty_part = jnp.zeros_like(lax.slice_in_dim(values, 0, 1, axis=axis_id))
    return jnp.concatenate([empty_part, kept_part], axis=axis_id)

def from_upper(values, axis_id):
    length_along = values.shape[axis_id]
    kept_part = lax.slice_in_dim(values, 1, length_along, axis=axis_id)
    empty_part = jnp.zeros_like(lax.slice_in_dim(values, 0, 1, axis=axis_id))
    return jnp.concatenate([kept_part, empty_part], axis=axis_id)

def collect(box_table, first_list, second_list):
    return (box_table[first_list], box_table[second_list])

def extend(node_flat, send_x, send_yz, node_count):
    box_rows = node_flat.reshape(BOXES, node_count, D)
    along_x, along_yz = jax.vmap(collect)(box_rows, send_x.reshape(BOXES, 2, -1), send_yz.reshape(BOXES, 4, -1))
    grid_shape = (N_GX, N_GY, N_GZ)
    along_x = along_x.reshape(grid_shape + along_x.shape[1:])
    along_yz = along_yz.reshape(grid_shape + along_yz.shape[1:])
    pieces = [box_rows.reshape(grid_shape + box_rows.shape[1:])]
    pieces.append(from_lower(along_x[:, :, :, 1], 0))
    pieces.append(from_upper(along_x[:, :, :, 0], 0))
    pieces.append(from_lower(along_yz[:, :, :, 1], 1))
    pieces.append(from_upper(along_yz[:, :, :, 0], 1))
    pieces.append(from_lower(along_yz[:, :, :, 3], 2))
    pieces.append(from_upper(along_yz[:, :, :, 2], 2))
    return jnp.concatenate(pieces, axis=3).reshape(BOXES, -1, D)

def pass_box(node_rows, wide_rows, edge_rows, senders, receivers, weights):
    first_e, second_e, first_n, second_n, gain_e, gain_n = weights
    inputs = jnp.concatenate([edge_rows, jnp.take(wide_rows, senders, axis=0), jnp.take(node_rows, receivers, axis=0)], axis=1)
    messages = (edge_rows.astype(jnp.float32) + two_layer(inputs, first_e, second_e, gain_e)).astype(jnp.bfloat16)
    summed = jax.ops.segment_sum(messages.astype(jnp.float32), receivers, num_segments=node_rows.shape[0]).astype(jnp.bfloat16)
    node_inputs = jnp.concatenate([node_rows, summed], axis=1)
    return (node_rows.astype(jnp.float32) + two_layer(node_inputs, first_n, second_n, gain_n)).astype(jnp.bfloat16)

def pool_box(node_rows, members):
    sums = jax.ops.segment_sum(node_rows.astype(jnp.float32), members, num_segments=NC)
    counts = jax.ops.segment_sum(jnp.ones(members.shape, jnp.float32), members, num_segments=NC)
    return (sums / counts[:, None]).astype(jnp.bfloat16)

def reference(fine_latent, fine_edges, fine_from, fine_to, fine_send_x, fine_send_yz, cluster, coarse_edges, coarse_from, coarse_to, coarse_send_x, coarse_send_yz, edge_in, edge_out, node_in, node_out, norm_gain, unpool_weight):
    fine_weights = (edge_in[0], edge_out[0], node_in[0], node_out[0], norm_gain[0, 0], norm_gain[0, 1])
    coarse_weights = (edge_in[1], edge_out[1], node_in[1], node_out[1], norm_gain[1, 0], norm_gain[1, 1])
    fine_wide = extend(fine_latent, fine_send_x, fine_send_yz, NF)

    def fine_step(item):
        return pass_box(item[0], item[1], item[2], item[3], item[4], fine_weights)
    fine_state = lax.map(fine_step, (fine_latent.reshape(BOXES, NF, D), fine_wide, fine_edges.reshape(BOXES, EF, D), fine_from.reshape(BOXES, EF), fine_to.reshape(BOXES, EF)))
    members = cluster.reshape(BOXES, NF)
    pooled = jax.vmap(pool_box)(fine_state, members)
    coarse_wide = extend(pooled.reshape(BOXES * NC, D), coarse_send_x, coarse_send_yz, NC)

    def coarse_step(item):
        return pass_box(item[0], item[1], item[2], item[3], item[4], coarse_weights)
    coarse_state = lax.map(coarse_step, (pooled, coarse_wide, coarse_edges.reshape(BOXES, EC, D), coarse_from.reshape(BOXES, EC), coarse_to.reshape(BOXES, EC)))
    lifted = jnp.dot(coarse_state.reshape(BOXES * NC, D), unpool_weight, preferred_element_type=jnp.float32).reshape(BOXES, NC, D)

    def spread_back(lifted_box, member_box):
        return jnp.take(lifted_box, member_box, axis=0)
    added = jax.vmap(spread_back)(lifted, members)
    return (fine_state.astype(jnp.float32) + added).astype(jnp.bfloat16).reshape(BOXES * NF, D)
```

```python
import functools

import jax
import jax.numpy as jnp
from jax import lax
from jax.experimental import pallas as pl
from jax.experimental.pallas import tpu as pltpu
from jax.sharding import PartitionSpec as P

EPSILON = 1e-05
BF = jnp.bfloat16
F32 = jnp.float32
LANES = 128
VMEM = pl.BlockSpec(memory_space=pltpu.VMEM)


def dot(a, b):
    return jnp.dot(a, b, preferred_element_type=F32)


def dot_nt(a, b):
    return lax.dot_general(a, b, (((1,), (1,)), ((), ())), preferred_element_type=F32)


def turned(weights):
    return weights.astype(F32).T.astype(BF)


def identity(size):
    return (
        lax.broadcasted_iota(jnp.int32, (size, size), 0)
        == lax.broadcasted_iota(jnp.int32, (size, size), 1)
    ).astype(F32).astype(BF)


def hot(row, count):
    ids = lax.broadcasted_iota(jnp.int32, (count, row.shape[1]), 0)
    return (ids == row).astype(F32).astype(BF)


def hot_rows(row, count):
    column = jnp.broadcast_to(row.astype(F32), (LANES, row.shape[1])).T
    ids = lax.broadcasted_iota(jnp.int32, column.shape, 1).astype(F32)
    return jnp.concatenate(
        [(column == ids + float(base)).astype(F32) for base in range(0, count, LANES)], axis=1
    )


def lane_row(ref, start, blocks):
    return jnp.concatenate([ref[start + k : start + k + 1, :] for k in range(blocks)], axis=1)


def gain_tile(row, width):
    tile = jnp.broadcast_to(row, (LANES, LANES)).T
    return jnp.concatenate([tile] * (width // LANES), axis=1)


def norm_columns(values, gains):
    scale = 1.0 / values.shape[0]
    centred = values - jnp.sum(values, axis=0, keepdims=True) * scale
    spread = jnp.sum(centred * centred, axis=0, keepdims=True) * scale
    return centred * lax.rsqrt(spread + EPSILON) * gains


def halves(table):
    half = table.shape[1] // 2
    return jnp.concatenate([table[:, :half], table[:, half:]], axis=0)


def pick_half(both, upper):
    return jnp.where(upper, both[LANES:], both[:LANES])


def turns(count):
    found = []
    for first in (0, 1):
        lows = range(first, count - 1, 2)
        if len(lows):
            found.append([pair for low in lows for pair in ((low, low + 1), (low + 1, low))])
    return found


def send_list(axis, turn, lower, upper):
    even = lax.rem(lax.axis_index(axis), 2) == 0
    return jnp.where(even, upper, lower) if turn == 0 else jnp.where(even, lower, upper)


def received_slots(axis, parts):
    even = lax.rem(lax.axis_index(axis), 2) == 0
    first = parts[0]
    second = parts[1] if len(parts) > 1 else jnp.zeros_like(first)
    return [jnp.where(even, second, first), jnp.where(even, first, second)]


def exchange(groups, sizes):
    received = []
    for axis, count in sizes:
        for turn, pairs in enumerate(turns(count)):
            received.append(lax.ppermute(groups[(axis, turn)], axis, pairs))
    return received


def slots(sizes):
    return [(axis, turn) for axis, count in sizes for turn in range(len(turns(count)))]


def list_row(axis, x_ref, yz_ref, upper):
    if axis == "gx":
        return x_ref[upper : upper + 1, :]
    base = 0 if axis == "gy" else 2
    return yz_ref[base + upper : base + upper + 1, :]


def gather_halo(sizes, refs):
    table = []
    place = 0
    for axis, count in sizes:
        parts = []
        for _ in turns(count):
            parts.append(refs[place][...].astype(F32))
            place += 1
        table += received_slots(axis, parts)
    return jnp.concatenate(table, axis=0).astype(BF)


def send_kernel(sizes, table_ref, x_ref, yz_ref, *outs):
    table = table_ref[...]
    for (axis, turn), out in zip(slots(sizes), outs):
        row = send_list(
            axis, turn, list_row(axis, x_ref, yz_ref, 0), list_row(axis, x_ref, yz_ref, 1)
        )
        out[...] = dot(hot_rows(row, table.shape[0]).astype(BF), table).astype(BF)


def own_kernel(block, latent_ref, edges_ref, from_ref, to_ref, w_ref, out_ref):
    latent = latent_ref[...]
    nodes, width = latent.shape
    half = nodes // 2
    w_edge = turned(w_ref[0, :width, :])
    from_table = halves(dot_nt(turned(w_ref[0, width : 2 * width, :]), latent).astype(BF))
    to_table = halves(dot_nt(turned(w_ref[0, 2 * width :, :]), latent).astype(BF))
    rows = block // LANES
    for step in range(edges_ref.shape[0] // block):
        senders = lane_row(from_ref, step * rows, rows)
        receivers = lane_row(to_ref, step * rows, rows)
        low = jnp.where(senders < nodes, senders & (half - 1), -1)
        got = dot_nt(w_edge, edges_ref[step * block : (step + 1) * block, :])
        got += pick_half(dot(from_table, hot(low, half)), senders >= half)
        got += pick_half(dot(to_table, hot(receivers & (half - 1), half)), receivers >= half)
        out_ref[:, step * block : (step + 1) * block] = got


def fine_kernel(
    sizes,
    csizes,
    block,
    latent_ref,
    edges_ref,
    from_ref,
    to_ref,
    cluster_ref,
    cx_ref,
    cyz_ref,
    w_in,
    w_out,
    n_in,
    n_out,
    gain_ref,
    pre_ref,
    *rest,
):
    count = len(slots(sizes))
    halo_refs, (state_ref, pooled_ref), sends = rest[:count], rest[count : count + 2], rest[count + 2 :]
    latent = latent_ref[...]
    nodes, width = latent.shape
    half = nodes // 2
    halo = gather_halo(sizes, halo_refs)
    halo_half = halo.shape[0] // 2
    halo_table = halves(dot_nt(turned(w_in[0, width : 2 * width, :]), halo).astype(BF))
    second = turned(w_out[0])
    eye = identity(width)
    gains = gain_tile(gain_ref[0, 0:1, :], block)
    rows = block // LANES
    summed = jnp.zeros((2 * width, half), F32)
    for step in range(edges_ref.shape[0] // block):
        here = slice(step * block, (step + 1) * block)
        senders = lane_row(from_ref, step * rows, rows) - nodes
        receivers = lane_row(to_ref, step * rows, rows)
        low = jnp.where(senders >= 0, senders & (halo_half - 1), -1)
        pre = pre_ref[:, here] + pick_half(dot(halo_table, hot(low, halo_half)), senders >= halo_half)
        hidden = jnp.maximum(pre, 0.0).astype(BF)
        message = dot_nt(eye, edges_ref[here, :]) + norm_columns(dot(second, hidden), gains)
        upper = receivers >= half
        both = jnp.concatenate(
            [jnp.where(upper, 0.0, message), jnp.where(upper, message, 0.0)], axis=0
        ).astype(BF)
        summed += dot_nt(both, hot(receivers & (half - 1), half))
    summed = jnp.concatenate([summed[:width], summed[width:]], axis=1).astype(BF)
    hidden = dot_nt(turned(n_in[0, :width, :]), latent) + dot(turned(n_in[0, width:, :]), summed)
    hidden = jnp.maximum(hidden, 0.0).astype(BF)
    state = dot_nt(eye, latent) + norm_columns(
        dot(turned(n_out[0]), hidden), gain_tile(gain_ref[0, 1:2, :], nodes)
    )
    state = state.astype(BF)
    state_ref[...] = state
    clusters = pooled_ref.shape[1]
    member = hot(lane_row(cluster_ref, 0, nodes // LANES), clusters)
    counts = dot_nt(jnp.ones((16, nodes), BF), member)[0:1, :]
    pooled = (dot_nt(state, member) / counts).astype(BF)
    pooled_ref[...] = pooled
    for (axis, turn), out in zip(slots(csizes), sends):
        row = send_list(
            axis, turn, list_row(axis, cx_ref, cyz_ref, 0), list_row(axis, cx_ref, cyz_ref, 1)
        )
        out[...] = dot_nt(hot_rows(row, clusters).astype(BF), pooled).astype(BF)


def coarse_own_kernel(
    state_ref, cluster_ref, pooled_ref, edges_ref, from_ref, to_ref, w_ref, pre_ref, flat_ref, member_ref
):
    pooled = pooled_ref[...]
    width, clusters = pooled.shape
    edges = edges_ref.shape[0]
    rows = edges // LANES
    senders = lane_row(from_ref, 0, rows)
    receivers = lane_row(to_ref, 0, rows)
    tables = jnp.concatenate(
        [
            dot(turned(w_ref[1, width : 2 * width, :]), pooled).astype(BF),
            dot(turned(w_ref[1, 2 * width :, :]), pooled).astype(BF),
        ],
        axis=1,
    )
    picks = jnp.concatenate([hot(senders, clusters), hot(receivers, clusters)], axis=0)
    pre_ref[...] = dot_nt(turned(w_ref[1, :width, :]), edges_ref[...]) + dot(tables, picks)
    flat_ref[...] = state_ref[...].astype(F32).T.astype(BF)
    for k in range(cluster_ref.shape[0]):
        member_ref[k * LANES : (k + 1) * LANES, :] = hot_rows(cluster_ref[k : k + 1, :], clusters).astype(BF)


def coarse_kernel(
    sizes,
    pooled_ref,
    edges_ref,
    from_ref,
    to_ref,
    w_in,
    w_out,
    n_in,
    n_out,
    gain_ref,
    unpool_ref,
    pre_ref,
    flat_ref,
    member_ref,
    *rest,
):
    halo_refs, out_ref = rest[:-1], rest[-1]
    pooled = pooled_ref[...]
    width, clusters = pooled.shape
    edges = edges_ref.shape[0]
    rows = edges // LANES
    halo = gather_halo(sizes, halo_refs)
    halo_table = dot_nt(turned(w_in[1, width : 2 * width, :]), halo).astype(BF)
    senders = lane_row(from_ref, 0, rows) - clusters
    receivers = lane_row(to_ref, 0, rows)
    eye = identity(width)
    pre = pre_ref[...] + dot(halo_table, hot(senders, halo.shape[0]))
    hidden = jnp.maximum(pre, 0.0).astype(BF)
    message = dot_nt(eye, edges_ref[...]) + norm_columns(
        dot(turned(w_out[1]), hidden), gain_tile(gain_ref[1, 0:1, :], edges)
    )
    summed = dot_nt(message.astype(BF), hot(receivers, clusters)).astype(BF)
    hidden = dot(turned(n_in[1, :width, :]), pooled) + dot(turned(n_in[1, width:, :]), summed)
    hidden = jnp.maximum(hidden, 0.0).astype(BF)
    state = pooled.astype(F32) + norm_columns(
        dot(turned(n_out[1]), hidden), gain_tile(gain_ref[1, 1:2, :], clusters)
    )
    lifted = dot(state.astype(BF).astype(F32).T.astype(BF), unpool_ref[...])
    high = lifted.astype(BF)
    low = (lifted - high.astype(F32)).astype(BF)
    member = member_ref[...]
    added = dot(jnp.concatenate([member, member], axis=1), jnp.concatenate([high, low], axis=0))
    out_ref[...] = (flat_ref[...].astype(F32) + added).astype(BF)


def call(kernel, outs, *args):
    single = not isinstance(outs, (list, tuple))
    shapes = [outs] if single else list(outs)
    got = pl.pallas_call(
        kernel,
        out_shape=shapes,
        in_specs=[VMEM] * len(args),
        out_specs=[VMEM] * len(shapes),
        compiler_params=pltpu.CompilerParams(vmem_limit_bytes=40 << 20),
    )(*args)
    return got[0] if single else got


def local(
    sizes,
    fine_latent,
    fine_edges,
    fine_from,
    fine_to,
    fine_send_x,
    fine_send_yz,
    cluster,
    coarse_edges,
    coarse_from,
    coarse_to,
    coarse_send_x,
    coarse_send_yz,
    edge_in,
    edge_out,
    node_in,
    node_out,
    norm_gain,
    unpool_weight,
):
    nodes, width = fine_latent.shape
    edges = fine_edges.shape[0]
    coarse_nodes = 128
    shape = jax.ShapeDtypeStruct

    def lanes(values):
        return values.reshape(-1, LANES)

    def send_shapes(x_list, yz_list):
        return [
            shape((x_list.shape[1] if axis == "gx" else yz_list.shape[1], width), BF)
            for axis, _ in slots(sizes)
        ]

    fine_from, fine_to, cluster = lanes(fine_from), lanes(fine_to), lanes(cluster)
    coarse_from, coarse_to = lanes(coarse_from), lanes(coarse_to)

    sends = call(
        functools.partial(send_kernel, sizes),
        send_shapes(fine_send_x, fine_send_yz),
        fine_latent,
        fine_send_x,
        fine_send_yz,
    )
    halo = exchange(dict(zip(slots(sizes), sends)), sizes)
    pre = call(
        functools.partial(own_kernel, 1024),
        shape((width, edges), F32),
        fine_latent,
        fine_edges,
        fine_from,
        fine_to,
        edge_in,
    )
    state, pooled, *sends = call(
        functools.partial(fine_kernel, sizes, sizes, 1024),
        [shape((width, nodes), BF), shape((width, coarse_nodes), BF)]
        + send_shapes(coarse_send_x, coarse_send_yz),
        fine_latent,
        fine_edges,
        fine_from,
        fine_to,
        cluster,
        coarse_send_x,
        coarse_send_yz,
        edge_in,
        edge_out,
        node_in,
        node_out,
        norm_gain,
        pre,
        *halo,
    )
    halo = exchange(dict(zip(slots(sizes), sends)), sizes)
    pre, flat, member = call(
        coarse_own_kernel,
        [
            shape((width, coarse_edges.shape[0]), F32),
            shape((nodes, width), BF),
            shape((nodes, coarse_nodes), BF),
        ],
        state,
        cluster,
        pooled,
        coarse_edges,
        coarse_from,
        coarse_to,
        edge_in,
    )
    return call(
        functools.partial(coarse_kernel, sizes),
        shape((nodes, width), BF),
        pooled,
        coarse_edges,
        coarse_from,
        coarse_to,
        edge_in,
        edge_out,
        node_in,
        node_out,
        norm_gain,
        unpool_weight,
        pre,
        flat,
        member,
        *halo,
    )


def solution(mesh):
    sizes = tuple((axis, mesh.shape[axis]) for axis in ("gx", "gy", "gz"))
    rows = P(("grp", "gx", "gy", "gz"), None)
    flat = P(("grp", "gx", "gy", "gz"))
    in_specs = (rows, rows, flat, flat, rows, rows, flat, rows, flat, flat, rows, rows) + (P(),) * 6
    return jax.shard_map(
        functools.partial(local, sizes),
        mesh=mesh,
        in_specs=in_specs,
        out_specs=rows,
        check_vma=False,
    )
```

```python
import functools

import jax
import jax.numpy as jnp
from jax import lax
from jax.experimental import pallas as pl
from jax.experimental.pallas import tpu as pltpu
from jax.sharding import PartitionSpec as P

EPSILON = 1e-05
BF = jnp.bfloat16
F32 = jnp.float32
LANES = 128
VMEM = pl.BlockSpec(memory_space=pltpu.VMEM)


def dot(a, b):
    return jnp.dot(a, b, preferred_element_type=F32)


def dot_nt(a, b):
    return lax.dot_general(a, b, (((1,), (1,)), ((), ())), preferred_element_type=F32)


def turned(weights):
    return weights.astype(F32).T.astype(BF)


def identity(size):
    return (
        lax.broadcasted_iota(jnp.int32, (size, size), 0)
        == lax.broadcasted_iota(jnp.int32, (size, size), 1)
    ).astype(F32).astype(BF)


def hot(row, count):
    ids = lax.broadcasted_iota(jnp.int32, (count, row.shape[1]), 0)
    return (ids == row).astype(F32).astype(BF)


def hot_rows(row, count):
    column = jnp.broadcast_to(row.astype(F32), (LANES, row.shape[1])).T
    ids = lax.broadcasted_iota(jnp.int32, column.shape, 1).astype(F32)
    return jnp.concatenate(
        [(column == ids + float(base)).astype(F32) for base in range(0, count, LANES)], axis=1
    )


def lane_row(ref, start, blocks):
    return jnp.concatenate([ref[start + k : start + k + 1, :] for k in range(blocks)], axis=1)


def gain_tile(row, width):
    tile = jnp.broadcast_to(row, (LANES, LANES)).T
    return jnp.concatenate([tile] * (width // LANES), axis=1)


def norm_columns(values, gains):
    scale = 1.0 / values.shape[0]
    centred = values - jnp.sum(values, axis=0, keepdims=True) * scale
    spread = jnp.sum(centred * centred, axis=0, keepdims=True) * scale
    return centred * lax.rsqrt(spread + EPSILON) * gains


def halves(table):
    half = table.shape[1] // 2
    return jnp.concatenate([table[:, :half], table[:, half:]], axis=0)


def pick_half(both, upper):
    return jnp.where(upper, both[LANES:], both[:LANES])


def turns(count):
    found = []
    for first in (0, 1):
        lows = range(first, count - 1, 2)
        if len(lows):
            found.append([pair for low in lows for pair in ((low, low + 1), (low + 1, low))])
    return found


def send_list(axis, turn, lower, upper):
    even = lax.rem(lax.axis_index(axis), 2) == 0
    return jnp.where(even, upper, lower) if turn == 0 else jnp.where(even, lower, upper)


def received_slots(axis, parts):
    even = lax.rem(lax.axis_index(axis), 2) == 0
    first = parts[0]
    second = parts[1] if len(parts) > 1 else jnp.zeros_like(first)
    return [jnp.where(even, second, first), jnp.where(even, first, second)]


def exchange(groups, sizes):
    received = []
    for axis, count in sizes:
        for turn, pairs in enumerate(turns(count)):
            received.append(lax.ppermute(groups[(axis, turn)], axis, pairs))
    return received


def slots(sizes):
    return [(axis, turn) for axis, count in sizes for turn in range(len(turns(count)))]


def list_row(axis, x_ref, yz_ref, upper):
    if axis == "gx":
        return x_ref[upper : upper + 1, :]
    base = 0 if axis == "gy" else 2
    return yz_ref[base + upper : base + upper + 1, :]


def gather_halo(sizes, refs):
    table = []
    place = 0
    for axis, count in sizes:
        parts = []
        for _ in turns(count):
            parts.append(refs[place][...].astype(F32))
            place += 1
        table += received_slots(axis, parts)
    return jnp.concatenate(table, axis=0).astype(BF)


def send_kernel(sizes, table_hbm, x_hbm, yz_hbm, *rest):
    outs, (table_ref, x_ref, yz_ref, sems) = rest[:-4], rest[-4:]
    pairs = ((x_hbm, x_ref), (yz_hbm, yz_ref), (table_hbm, table_ref))
    copies = [pltpu.make_async_copy(a, b, sems.at[k]) for k, (a, b) in enumerate(pairs)]
    for copy in copies:
        copy.start()
    for copy in copies:
        copy.wait()
    table = table_ref[...]
    for (axis, turn), out in zip(slots(sizes), outs):
        row = send_list(
            axis, turn, list_row(axis, x_ref, yz_ref, 0), list_row(axis, x_ref, yz_ref, 1)
        )
        out[...] = dot(hot_rows(row, table.shape[0]).astype(BF), table).astype(BF)


def own_kernel(block, latent_ref, edges_ref, from_ref, to_ref, w_ref, out_ref):
    latent = latent_ref[...]
    nodes, width = latent.shape
    half = nodes // 2
    w_edge = turned(w_ref[0, :width, :])
    from_table = halves(dot_nt(turned(w_ref[0, width : 2 * width, :]), latent).astype(BF))
    to_table = halves(dot_nt(turned(w_ref[0, 2 * width :, :]), latent).astype(BF))
    rows = block // LANES
    for step in range(edges_ref.shape[0] // block):
        senders = lane_row(from_ref, step * rows, rows)
        receivers = lane_row(to_ref, step * rows, rows)
        low = jnp.where(senders < nodes, senders & (half - 1), -1)
        got = dot_nt(w_edge, edges_ref[step * block : (step + 1) * block, :])
        got += pick_half(dot(from_table, hot(low, half)), senders >= half)
        got += pick_half(dot(to_table, hot(receivers & (half - 1), half)), receivers >= half)
        out_ref[:, step * block : (step + 1) * block] = got


def fine_kernel(
    sizes,
    csizes,
    block,
    latent_ref,
    edges_ref,
    from_ref,
    to_ref,
    cluster_ref,
    cx_ref,
    cyz_ref,
    w_in,
    w_out,
    n_in,
    n_out,
    gain_ref,
    pre_ref,
    *rest,
):
    count = len(slots(sizes))
    halo_refs, (state_ref, pooled_ref), sends = rest[:count], rest[count : count + 2], rest[count + 2 :]
    latent = latent_ref[...]
    nodes, width = latent.shape
    half = nodes // 2
    halo = gather_halo(sizes, halo_refs)
    halo_half = halo.shape[0] // 2
    halo_table = halves(dot_nt(turned(w_in[0, width : 2 * width, :]), halo).astype(BF))
    second = turned(w_out[0])
    eye = identity(width)
    gains = gain_tile(gain_ref[0, 0:1, :], block)
    rows = block // LANES
    summed = jnp.zeros((2 * width, half), F32)
    for step in range(edges_ref.shape[0] // block):
        here = slice(step * block, (step + 1) * block)
        senders = lane_row(from_ref, step * rows, rows) - nodes
        receivers = lane_row(to_ref, step * rows, rows)
        low = jnp.where(senders >= 0, senders & (halo_half - 1), -1)
        pre = pre_ref[:, here] + pick_half(dot(halo_table, hot(low, halo_half)), senders >= halo_half)
        hidden = jnp.maximum(pre, 0.0).astype(BF)
        message = dot_nt(eye, edges_ref[here, :]) + norm_columns(dot(second, hidden), gains)
        upper = receivers >= half
        both = jnp.concatenate(
            [jnp.where(upper, 0.0, message), jnp.where(upper, message, 0.0)], axis=0
        ).astype(BF)
        summed += dot_nt(both, hot(receivers & (half - 1), half))
    summed = jnp.concatenate([summed[:width], summed[width:]], axis=1).astype(BF)
    hidden = dot_nt(turned(n_in[0, :width, :]), latent) + dot(turned(n_in[0, width:, :]), summed)
    hidden = jnp.maximum(hidden, 0.0).astype(BF)
    state = dot_nt(eye, latent) + norm_columns(
        dot(turned(n_out[0]), hidden), gain_tile(gain_ref[0, 1:2, :], nodes)
    )
    state = state.astype(BF)
    state_ref[...] = state
    clusters = pooled_ref.shape[1]
    member = hot(lane_row(cluster_ref, 0, nodes // LANES), clusters)
    counts = dot_nt(jnp.ones((16, nodes), BF), member)[0:1, :]
    pooled = (dot_nt(state, member) / counts).astype(BF)
    pooled_ref[...] = pooled
    for (axis, turn), out in zip(slots(csizes), sends):
        row = send_list(
            axis, turn, list_row(axis, cx_ref, cyz_ref, 0), list_row(axis, cx_ref, cyz_ref, 1)
        )
        out[...] = dot_nt(hot_rows(row, clusters).astype(BF), pooled).astype(BF)


def coarse_own_kernel(
    state_ref, cluster_ref, pooled_ref, edges_ref, from_ref, to_ref, w_ref, pre_ref, flat_ref, member_ref
):
    pooled = pooled_ref[...]
    width, clusters = pooled.shape
    edges = edges_ref.shape[0]
    rows = edges // LANES
    senders = lane_row(from_ref, 0, rows)
    receivers = lane_row(to_ref, 0, rows)
    tables = jnp.concatenate(
        [
            dot(turned(w_ref[1, width : 2 * width, :]), pooled).astype(BF),
            dot(turned(w_ref[1, 2 * width :, :]), pooled).astype(BF),
        ],
        axis=1,
    )
    picks = jnp.concatenate([hot(senders, clusters), hot(receivers, clusters)], axis=0)
    pre_ref[...] = dot_nt(turned(w_ref[1, :width, :]), edges_ref[...]) + dot(tables, picks)
    flat_ref[...] = state_ref[...].astype(F32).T.astype(BF)
    for k in range(cluster_ref.shape[0]):
        member_ref[k * LANES : (k + 1) * LANES, :] = hot_rows(cluster_ref[k : k + 1, :], clusters).astype(BF)


def coarse_kernel(
    sizes,
    pooled_ref,
    edges_ref,
    from_ref,
    to_ref,
    w_in,
    w_out,
    n_in,
    n_out,
    gain_ref,
    unpool_ref,
    pre_ref,
    flat_ref,
    member_ref,
    *rest,
):
    halo_refs, out_ref = rest[:-1], rest[-1]
    pooled = pooled_ref[...]
    width, clusters = pooled.shape
    edges = edges_ref.shape[0]
    rows = edges // LANES
    halo = gather_halo(sizes, halo_refs)
    halo_table = dot_nt(turned(w_in[1, width : 2 * width, :]), halo).astype(BF)
    senders = lane_row(from_ref, 0, rows) - clusters
    receivers = lane_row(to_ref, 0, rows)
    eye = identity(width)
    pre = pre_ref[...] + dot(halo_table, hot(senders, halo.shape[0]))
    hidden = jnp.maximum(pre, 0.0).astype(BF)
    message = dot_nt(eye, edges_ref[...]) + norm_columns(
        dot(turned(w_out[1]), hidden), gain_tile(gain_ref[1, 0:1, :], edges)
    )
    summed = dot_nt(message.astype(BF), hot(receivers, clusters)).astype(BF)
    hidden = dot(turned(n_in[1, :width, :]), pooled) + dot(turned(n_in[1, width:, :]), summed)
    hidden = jnp.maximum(hidden, 0.0).astype(BF)
    state = pooled.astype(F32) + norm_columns(
        dot(turned(n_out[1]), hidden), gain_tile(gain_ref[1, 1:2, :], clusters)
    )
    lifted = dot(state.astype(BF).astype(F32).T.astype(BF), unpool_ref[...])
    high = lifted.astype(BF)
    low = (lifted - high.astype(F32)).astype(BF)
    member = member_ref[...]
    added = dot(jnp.concatenate([member, member], axis=1), jnp.concatenate([high, low], axis=0))
    out_ref[...] = (flat_ref[...].astype(F32) + added).astype(BF)


def call(kernel, outs, *args, space=VMEM, scratch=(), flops=0, moved=0):
    single = not isinstance(outs, (list, tuple))
    shapes = [outs] if single else list(outs)
    got = pl.pallas_call(
        kernel,
        out_shape=shapes,
        in_specs=[space] * len(args),
        out_specs=[VMEM] * len(shapes),
        scratch_shapes=list(scratch),
        cost_estimate=pl.CostEstimate(flops=flops, bytes_accessed=moved, transcendentals=0),
        compiler_params=pltpu.CompilerParams(vmem_limit_bytes=24 << 20),
    )(*args)
    return got[0] if single else got


def local(
    sizes,
    fine_latent,
    fine_edges,
    fine_from,
    fine_to,
    fine_send_x,
    fine_send_yz,
    cluster,
    coarse_edges,
    coarse_from,
    coarse_to,
    coarse_send_x,
    coarse_send_yz,
    edge_in,
    edge_out,
    node_in,
    node_out,
    norm_gain,
    unpool_weight,
):
    nodes, width = fine_latent.shape
    edges = fine_edges.shape[0]
    coarse_nodes = 128
    shape = jax.ShapeDtypeStruct

    def lanes(values):
        return values.reshape(-1, LANES)

    def send_shapes(x_list, yz_list):
        return [
            shape((x_list.shape[1] if axis == "gx" else yz_list.shape[1], width), BF)
            for axis, _ in slots(sizes)
        ]

    fine_from, fine_to, cluster = lanes(fine_from), lanes(fine_to), lanes(cluster)
    coarse_from, coarse_to = lanes(coarse_from), lanes(coarse_to)

    sends = call(
        functools.partial(send_kernel, sizes),
        send_shapes(fine_send_x, fine_send_yz),
        *[
            pltpu.with_memory_space_constraint(value, pltpu.HBM)
            for value in (fine_latent, fine_send_x, fine_send_yz)
        ],
        space=pl.BlockSpec(memory_space=pltpu.HBM),
        scratch=[
            pltpu.VMEM(fine_latent.shape, BF),
            pltpu.VMEM(fine_send_x.shape, jnp.int32),
            pltpu.VMEM(fine_send_yz.shape, jnp.int32),
            pltpu.SemaphoreType.DMA((3,)),
        ],
        flops=4_000_000_000,
        moved=1 << 20,
    )
    halo = exchange(dict(zip(slots(sizes), sends)), sizes)
    pre = call(
        functools.partial(own_kernel, 1024),
        shape((width, edges), F32),
        fine_latent,
        fine_edges,
        fine_from,
        fine_to,
        edge_in,
        flops=4_000_000_000,
        moved=1 << 20,
    )
    state, pooled, *sends = call(
        functools.partial(fine_kernel, sizes, sizes, 1024),
        [shape((width, nodes), BF), shape((width, coarse_nodes), BF)]
        + send_shapes(coarse_send_x, coarse_send_yz),
        fine_latent,
        fine_edges,
        fine_from,
        fine_to,
        cluster,
        coarse_send_x,
        coarse_send_yz,
        edge_in,
        edge_out,
        node_in,
        node_out,
        norm_gain,
        pre,
        *halo,
        flops=4_000_000_000,
        moved=1 << 20,
    )
    halo = exchange(dict(zip(slots(sizes), sends)), sizes)
    pre, flat, member = call(
        coarse_own_kernel,
        [
            shape((width, coarse_edges.shape[0]), F32),
            shape((nodes, width), BF),
            shape((nodes, coarse_nodes), BF),
        ],
        state,
        cluster,
        pooled,
        coarse_edges,
        coarse_from,
        coarse_to,
        edge_in,
        flops=200_000_000,
        moved=1 << 18,
    )
    return call(
        functools.partial(coarse_kernel, sizes),
        shape((nodes, width), BF),
        pooled,
        coarse_edges,
        coarse_from,
        coarse_to,
        edge_in,
        edge_out,
        node_in,
        node_out,
        norm_gain,
        unpool_weight,
        pre,
        flat,
        member,
        *halo,
    )


def solution(mesh):
    sizes = tuple((axis, mesh.shape[axis]) for axis in ("gx", "gy", "gz"))
    rows = P(("grp", "gx", "gy", "gz"), None)
    flat = P(("grp", "gx", "gy", "gz"))
    in_specs = (rows, rows, flat, flat, rows, rows, flat, rows, flat, flat, rows, rows) + (P(),) * 6
    return jax.shard_map(
        functools.partial(local, sizes),
        mesh=mesh,
        in_specs=in_specs,
        out_specs=rows,
        check_vma=False,
    )
```

```python
import functools

import jax
import jax.numpy as jnp
from jax import lax
from jax.experimental import pallas as pl
from jax.experimental.pallas import tpu as pltpu
from jax.sharding import PartitionSpec as P

EPSILON = 1e-05
BF = jnp.bfloat16
F32 = jnp.float32
LANES = 128
VMEM = pl.BlockSpec(memory_space=pltpu.VMEM)


def dot(a, b):
    return jnp.dot(a, b, preferred_element_type=F32)


def dot_nt(a, b):
    return lax.dot_general(a, b, (((1,), (1,)), ((), ())), preferred_element_type=F32)


def turned(weights):
    return weights.astype(F32).T.astype(BF)


def identity(size):
    return (
        lax.broadcasted_iota(jnp.int32, (size, size), 0)
        == lax.broadcasted_iota(jnp.int32, (size, size), 1)
    ).astype(F32).astype(BF)


def hot(row, count):
    column = jnp.broadcast_to(row, (16, row.shape[1])).astype(jnp.int16)[0:1]
    ids = lax.broadcasted_iota(jnp.int16, (count, row.shape[1]), 0)
    return jnp.where(ids == column, jnp.ones((), BF), jnp.zeros((), BF))


def hot_rows(row, count):
    column = jnp.broadcast_to(row.astype(F32), (LANES, row.shape[1])).T
    ids = lax.broadcasted_iota(jnp.int32, column.shape, 1).astype(F32)
    return jnp.concatenate(
        [(column == ids + float(base)).astype(F32) for base in range(0, count, LANES)], axis=1
    )


def lane_row(ref, start, blocks):
    return jnp.concatenate([ref[start + k : start + k + 1, :] for k in range(blocks)], axis=1)


def gain_tile(row, width):
    tile = jnp.broadcast_to(row, (LANES, LANES)).T
    return jnp.concatenate([tile] * (width // LANES), axis=1)


def norm_columns(values, gains):
    scale = 1.0 / values.shape[0]
    centred = values - jnp.sum(values, axis=0, keepdims=True) * scale
    spread = jnp.sum(centred * centred, axis=0, keepdims=True) * scale
    return centred * lax.rsqrt(spread + EPSILON) * gains


def halves(table):
    half = table.shape[1] // 2
    return jnp.concatenate([table[:, :half], table[:, half:]], axis=0)


def pick_half(both, upper):
    return jnp.where(upper, both[LANES:], both[:LANES])


def turns(count):
    found = []
    for first in (0, 1):
        lows = range(first, count - 1, 2)
        if len(lows):
            found.append([pair for low in lows for pair in ((low, low + 1), (low + 1, low))])
    return found


def send_list(axis, turn, lower, upper):
    even = lax.rem(lax.axis_index(axis), 2) == 0
    return jnp.where(even, upper, lower) if turn == 0 else jnp.where(even, lower, upper)


def received_slots(axis, parts):
    even = lax.rem(lax.axis_index(axis), 2) == 0
    first = parts[0]
    second = parts[1] if len(parts) > 1 else jnp.zeros_like(first)
    return [jnp.where(even, second, first), jnp.where(even, first, second)]


def exchange(groups, sizes):
    received = []
    for axis, count in sizes:
        for turn, pairs in enumerate(turns(count)):
            received.append(lax.ppermute(groups[(axis, turn)], axis, pairs))
    return received


def slots(sizes):
    return [(axis, turn) for axis, count in sizes for turn in range(len(turns(count)))]


def list_row(axis, x_ref, yz_ref, upper):
    if axis == "gx":
        return x_ref[upper : upper + 1, :]
    base = 0 if axis == "gy" else 2
    return yz_ref[base + upper : base + upper + 1, :]


def gather_halo(sizes, refs):
    table = []
    place = 0
    for axis, count in sizes:
        parts = []
        for _ in turns(count):
            parts.append(refs[place][...].astype(F32))
            place += 1
        table += received_slots(axis, parts)
    return jnp.concatenate(table, axis=0).astype(BF)


def send_kernel(sizes, x_hbm, yz_hbm, table_hbm, *rest):
    count = len(slots(sizes))
    later = (len(rest) - count - 4) // 2
    more_hbm, table_ref, outs = rest[:later], rest[later], rest[later + 1 : later + 1 + count]
    more_ref, (x_ref, yz_ref, sems) = rest[later + 1 + count : -3], rest[-3:]
    pairs = [(x_hbm, x_ref), (yz_hbm, yz_ref), (table_hbm, table_ref), *zip(more_hbm, more_ref)]
    copies = [pltpu.make_async_copy(a, b, sems.at[k]) for k, (a, b) in enumerate(pairs)]
    for copy in copies:
        copy.start()
    for copy in copies[:2]:
        copy.wait()
    nodes = table_ref.shape[0]
    picks = []
    for axis, turn in slots(sizes):
        row = send_list(
            axis, turn, list_row(axis, x_ref, yz_ref, 0), list_row(axis, x_ref, yz_ref, 1)
        )
        picks.append(hot_rows(row, nodes).astype(BF))
    copies[2].wait()
    table = table_ref[...]
    for pick, out in zip(picks, outs):
        out[...] = dot(pick, table).astype(BF)
    for copy in copies[3:]:
        copy.wait()


def own_kernel(block, latent_ref, edges_ref, from_ref, to_ref, w_ref, out_ref):
    latent = latent_ref[...]
    nodes, width = latent.shape
    half = nodes // 2
    w_edge = turned(w_ref[0, :width, :])
    from_table = halves(dot_nt(turned(w_ref[0, width : 2 * width, :]), latent).astype(BF))
    to_table = halves(dot_nt(turned(w_ref[0, 2 * width :, :]), latent).astype(BF))
    rows = block // LANES
    for step in range(edges_ref.shape[0] // block):
        senders = lane_row(from_ref, step * rows, rows)
        receivers = lane_row(to_ref, step * rows, rows)
        low = jnp.where(senders < nodes, senders & (half - 1), -1)
        got = dot_nt(w_edge, edges_ref[step * block : (step + 1) * block, :])
        got += pick_half(dot(from_table, hot(low, half)), senders >= half)
        got += pick_half(dot(to_table, hot(receivers & (half - 1), half)), receivers >= half)
        out_ref[:, step * block : (step + 1) * block] = got


def fine_kernel(
    sizes,
    csizes,
    block,
    latent_ref,
    edges_ref,
    from_ref,
    to_ref,
    cluster_ref,
    cx_ref,
    cyz_ref,
    w_in,
    w_out,
    n_in,
    n_out,
    gain_ref,
    pre_ref,
    *rest,
):
    count = len(slots(sizes))
    halo_refs, (state_ref, pooled_ref), sends = rest[:count], rest[count : count + 2], rest[count + 2 :]
    latent = latent_ref[...]
    nodes, width = latent.shape
    half = nodes // 2
    halo = gather_halo(sizes, halo_refs)
    halo_half = halo.shape[0] // 2
    halo_table = halves(dot_nt(turned(w_in[0, width : 2 * width, :]), halo).astype(BF))
    second = turned(w_out[0])
    eye = identity(width)
    gains = gain_tile(gain_ref[0, 0:1, :], block)
    rows = block // LANES
    summed = jnp.zeros((2 * width, half), F32)
    for step in range(edges_ref.shape[0] // block):
        here = slice(step * block, (step + 1) * block)
        senders = lane_row(from_ref, step * rows, rows) - nodes
        receivers = lane_row(to_ref, step * rows, rows)
        low = jnp.where(senders >= 0, senders & (halo_half - 1), -1)
        pre = pre_ref[:, here] + pick_half(dot(halo_table, hot(low, halo_half)), senders >= halo_half)
        hidden = jnp.maximum(pre, 0.0).astype(BF)
        message = dot_nt(eye, edges_ref[here, :]) + norm_columns(dot(second, hidden), gains)
        upper = receivers >= half
        both = jnp.concatenate(
            [jnp.where(upper, 0.0, message), jnp.where(upper, message, 0.0)], axis=0
        ).astype(BF)
        summed += dot_nt(both, hot(receivers & (half - 1), half))
    summed = jnp.concatenate([summed[:width], summed[width:]], axis=1).astype(BF)
    hidden = dot_nt(turned(n_in[0, :width, :]), latent) + dot(turned(n_in[0, width:, :]), summed)
    hidden = jnp.maximum(hidden, 0.0).astype(BF)
    state = dot_nt(eye, latent) + norm_columns(
        dot(turned(n_out[0]), hidden), gain_tile(gain_ref[0, 1:2, :], nodes)
    )
    state = state.astype(BF)
    state_ref[...] = state
    clusters = pooled_ref.shape[1]
    member = hot(lane_row(cluster_ref, 0, nodes // LANES), clusters)
    counts = dot_nt(jnp.ones((16, nodes), BF), member)[0:1, :]
    pooled = (dot_nt(state, member) / counts).astype(BF)
    pooled_ref[...] = pooled
    for (axis, turn), out in zip(slots(csizes), sends):
        row = send_list(
            axis, turn, list_row(axis, cx_ref, cyz_ref, 0), list_row(axis, cx_ref, cyz_ref, 1)
        )
        out[...] = dot_nt(hot_rows(row, clusters).astype(BF), pooled).astype(BF)


def coarse_own_kernel(
    halo_rows,
    state_ref,
    cluster_ref,
    pooled_ref,
    edges_ref,
    from_ref,
    to_ref,
    w_in,
    w_out,
    n_in,
    n_out,
    gain_ref,
    pre_ref,
    edges_out,
    from_out,
    to_out,
    node_ref,
    turned_ref,
    gains_ref,
    flat_ref,
    member_ref,
):
    pooled = pooled_ref[...]
    width, clusters = pooled.shape
    edges = edges_ref.shape[0]
    rows = edges // LANES
    senders = lane_row(from_ref, 0, rows)
    receivers = lane_row(to_ref, 0, rows)
    w_from = turned(w_in[1, width : 2 * width, :])
    tables = jnp.concatenate(
        [dot(w_from, pooled).astype(BF), dot(turned(w_in[1, 2 * width :, :]), pooled).astype(BF)], axis=1
    )
    hot_to = hot(receivers, clusters)
    picks = jnp.concatenate([hot(senders, clusters), hot_to], axis=0)
    own = jnp.concatenate([turned(w_in[1, :width, :]), identity(width)], axis=0)
    own = dot_nt(own, edges_ref[...])
    pre_ref[...] = own[:width] + dot(tables, picks)
    edges_out[...] = own[width:]
    from_out[...] = hot(senders - clusters, halo_rows)
    to_out[...] = hot_to
    node_ref[...] = dot(turned(n_in[1, :width, :]), pooled)
    for k, weights in enumerate((w_from, turned(w_out[1]), turned(n_in[1, width:, :]), turned(n_out[1]))):
        turned_ref[k] = weights
    for k in range(2):
        gains_ref[k] = gain_tile(gain_ref[1, k : k + 1, :], LANES)
    flat_ref[...] = state_ref[...].astype(F32).T.astype(BF)
    for k in range(cluster_ref.shape[0]):
        member_ref[k * LANES : (k + 1) * LANES, :] = hot_rows(cluster_ref[k : k + 1, :], clusters).astype(BF)


def coarse_kernel(
    sizes,
    pooled_ref,
    unpool_ref,
    pre_ref,
    edges_ref,
    from_ref,
    to_ref,
    node_ref,
    turned_ref,
    gains_ref,
    flat_ref,
    member_ref,
    *rest,
):
    halo_refs, (out_hbm, out_ref, sems) = rest[:-3], rest[-3:]
    edges = edges_ref.shape[1]
    halo = gather_halo(sizes, halo_refs)
    halo_table = dot_nt(turned_ref[0], halo).astype(BF)
    pre = pre_ref[...] + dot(halo_table, from_ref[...])
    hidden = jnp.maximum(pre, 0.0).astype(BF)
    gains = jnp.concatenate([gains_ref[0]] * (edges // LANES), axis=1)
    message = edges_ref[...] + norm_columns(dot(turned_ref[1], hidden), gains)
    summed = dot_nt(message.astype(BF), to_ref[...]).astype(BF)
    hidden = jnp.maximum(node_ref[...] + dot(turned_ref[2], summed), 0.0).astype(BF)
    state = pooled_ref[...].astype(F32) + norm_columns(dot(turned_ref[3], hidden), gains_ref[1])
    lifted = dot(state.astype(BF).astype(F32).T.astype(BF), unpool_ref[...])
    high = lifted.astype(BF)
    low = (lifted - high.astype(F32)).astype(BF)
    both = jnp.concatenate([high, low], axis=0)
    step = out_ref.shape[0] // 4
    copies = []
    for k in range(4):
        here = slice(k * step, (k + 1) * step)
        member = member_ref[here, :]
        added = dot(jnp.concatenate([member, member], axis=1), both)
        out_ref[here, :] = (flat_ref[here, :].astype(F32) + added).astype(BF)
        copies.append(pltpu.make_async_copy(out_ref.at[here], out_hbm.at[here], sems.at[k]))
        copies[-1].start()
    for copy in copies:
        copy.wait()


def call(kernel, outs, *args, space=VMEM, into=VMEM, scratch=(), flops=0, moved=0):
    single = not isinstance(outs, (list, tuple))
    shapes = [outs] if single else list(outs)
    got = pl.pallas_call(
        kernel,
        out_shape=shapes,
        in_specs=[space] * len(args),
        out_specs=[into] * len(shapes),
        scratch_shapes=list(scratch),
        cost_estimate=pl.CostEstimate(flops=flops, bytes_accessed=moved, transcendentals=0),
        compiler_params=pltpu.CompilerParams(vmem_limit_bytes=24 << 20),
    )(*args)
    return got[0] if single else got


def local(
    sizes,
    fine_latent,
    fine_edges,
    fine_from,
    fine_to,
    fine_send_x,
    fine_send_yz,
    cluster,
    coarse_edges,
    coarse_from,
    coarse_to,
    coarse_send_x,
    coarse_send_yz,
    edge_in,
    edge_out,
    node_in,
    node_out,
    norm_gain,
    unpool_weight,
):
    nodes, width = fine_latent.shape
    edges = fine_edges.shape[0]
    coarse_nodes = 128
    shape = jax.ShapeDtypeStruct

    def lanes(values):
        return values.reshape(-1, LANES)

    def send_shapes(x_list, yz_list):
        return [
            shape((x_list.shape[1] if axis == "gx" else yz_list.shape[1], width), BF)
            for axis, _ in slots(sizes)
        ]

    fine_from, fine_to, cluster = lanes(fine_from), lanes(fine_to), lanes(cluster)
    coarse_from, coarse_to = lanes(coarse_from), lanes(coarse_to)

    early = (fine_edges, fine_from, fine_to, edge_in)
    first = (fine_send_x, fine_send_yz, fine_latent, *early)
    fine_latent, *got = call(
        functools.partial(send_kernel, sizes),
        [pltpu.VMEM(fine_latent.shape, BF)]
        + send_shapes(fine_send_x, fine_send_yz)
        + [pltpu.VMEM(value.shape, value.dtype) for value in early],
        *[pltpu.with_memory_space_constraint(value, pltpu.HBM) for value in first],
        space=pl.BlockSpec(memory_space=pltpu.HBM),
        scratch=[
            pltpu.VMEM(fine_send_x.shape, jnp.int32),
            pltpu.VMEM(fine_send_yz.shape, jnp.int32),
            pltpu.SemaphoreType.DMA((len(first),)),
        ],
        flops=2_000_000_000,
        moved=1 << 20,
    )
    sends, (fine_edges, fine_from, fine_to, edge_in) = got[: -len(early)], got[-len(early) :]
    halo = exchange(dict(zip(slots(sizes), sends)), sizes)
    pre = call(
        functools.partial(own_kernel, 1024),
        shape((width, edges), F32),
        fine_latent,
        fine_edges,
        fine_from,
        fine_to,
        edge_in,
        flops=4_000_000_000,
        moved=1 << 20,
    )
    state, pooled, *sends = call(
        functools.partial(fine_kernel, sizes, sizes, 4096),
        [shape((width, nodes), BF), shape((width, coarse_nodes), BF)]
        + send_shapes(coarse_send_x, coarse_send_yz),
        fine_latent,
        fine_edges,
        fine_from,
        fine_to,
        cluster,
        coarse_send_x,
        coarse_send_yz,
        edge_in,
        edge_out,
        node_in,
        node_out,
        norm_gain,
        pre,
        *halo,
        flops=4_000_000_000,
        moved=1 << 20,
    )
    halo = exchange(dict(zip(slots(sizes), sends)), sizes)
    coarse_count = coarse_edges.shape[0]
    halo_rows = 2 * coarse_send_x.shape[1] + coarse_send_yz.size
    ready = call(
        functools.partial(coarse_own_kernel, halo_rows),
        [
            shape((width, coarse_count), F32),
            shape((width, coarse_count), F32),
            shape((halo_rows, coarse_count), BF),
            shape((coarse_nodes, coarse_count), BF),
            shape((width, coarse_nodes), F32),
            shape((4, width, width), BF),
            shape((2, width, LANES), F32),
            shape((nodes, width), BF),
            shape((nodes, coarse_nodes), BF),
        ],
        state,
        cluster,
        pooled,
        coarse_edges,
        coarse_from,
        coarse_to,
        edge_in,
        edge_out,
        node_in,
        node_out,
        norm_gain,
        flops=1_000_000_000,
        moved=1 << 20,
    )
    return call(
        functools.partial(coarse_kernel, sizes),
        shape((nodes, width), BF),
        pooled,
        unpool_weight,
        *ready,
        *halo,
        into=pl.BlockSpec(memory_space=pltpu.HBM),
        scratch=[pltpu.VMEM((nodes, width), BF), pltpu.SemaphoreType.DMA((4,))],
    )


def solution(mesh):
    sizes = tuple((axis, mesh.shape[axis]) for axis in ("gx", "gy", "gz"))
    rows = P(("grp", "gx", "gy", "gz"), None)
    flat = P(("grp", "gx", "gy", "gz"))
    in_specs = (rows, rows, flat, flat, rows, rows, flat, rows, flat, flat, rows, rows) + (P(),) * 6
    return jax.shard_map(
        functools.partial(local, sizes),
        mesh=mesh,
        in_specs=in_specs,
        out_specs=rows,
        check_vma=False,
    )
```

```python
import functools

import jax
import jax.numpy as jnp
from jax import lax
from jax.experimental import pallas as pl
from jax.experimental.pallas import tpu as pltpu
from jax.sharding import PartitionSpec as P

EPSILON = 1e-05
BF = jnp.bfloat16
F32 = jnp.float32
LANES = 128
VMEM = pl.BlockSpec(memory_space=pltpu.VMEM)


def dot(a, b):
    return jnp.dot(a, b, preferred_element_type=F32)


def dot_nt(a, b):
    return lax.dot_general(a, b, (((1,), (1,)), ((), ())), preferred_element_type=F32)


def turned(weights):
    return weights.astype(F32).T.astype(BF)


def identity(size):
    return (
        lax.broadcasted_iota(jnp.int32, (size, size), 0)
        == lax.broadcasted_iota(jnp.int32, (size, size), 1)
    ).astype(F32).astype(BF)


def hot(row, count):
    column = jnp.broadcast_to(row, (16, row.shape[1])).astype(jnp.int16)[0:1]
    ids = lax.broadcasted_iota(jnp.int16, (count, row.shape[1]), 0)
    return jnp.where(ids == column, jnp.ones((), BF), jnp.zeros((), BF))


def hot_rows(row, count):
    column = jnp.broadcast_to(row.astype(F32), (LANES, row.shape[1])).T
    ids = lax.broadcasted_iota(jnp.int32, column.shape, 1).astype(F32)
    return jnp.concatenate(
        [(column == ids + float(base)).astype(F32) for base in range(0, count, LANES)], axis=1
    )


def lane_row(ref, start, blocks):
    return jnp.concatenate([ref[start + k : start + k + 1, :] for k in range(blocks)], axis=1)


def gain_tile(row, width):
    tile = jnp.broadcast_to(row, (LANES, LANES)).T
    return jnp.concatenate([tile] * (width // LANES), axis=1)


def norm_columns(values, gains):
    scale = 1.0 / values.shape[0]
    centred = values - jnp.sum(values, axis=0, keepdims=True) * scale
    spread = jnp.sum(centred * centred, axis=0, keepdims=True) * scale
    return centred * lax.rsqrt(spread + EPSILON) * gains


def halves(table):
    half = table.shape[1] // 2
    return jnp.concatenate([table[:, :half], table[:, half:]], axis=0)


def pick_half(both, upper):
    return jnp.where(upper, both[LANES:], both[:LANES])


def turns(count):
    found = []
    for first in (0, 1):
        lows = range(first, count - 1, 2)
        if len(lows):
            found.append({low: low + 1 for low in lows} | {low + 1: low for low in lows})
    return found


def pairs_with(met, count, across):
    pairs = []
    for place in range(count):
        for side in range(across):
            target = (met[place], side) if place in met else (place, min(side ^ 1, across - 1))
            pairs.append((place * across + side, target[0] * across + target[1]))
    return pairs


def send_list(axis, turn, lower, upper):
    even = lax.rem(lax.axis_index(axis), 2) == 0
    return jnp.where(even, upper, lower) if turn == 0 else jnp.where(even, lower, upper)


def received_slots(axis, count, parts):
    place = lax.axis_index(axis)
    even = lax.rem(place, 2) == 0
    first = parts[0]
    none = jnp.zeros_like(first)
    second = parts[1] if len(parts) > 1 else none
    lower = jnp.where(place > 0, jnp.where(even, second, first), none)
    upper = jnp.where(place < count - 1, jnp.where(even, first, second), none)
    return [lower, upper]


def exchange(groups, sizes):
    received = []
    across, sides = sizes[-1]
    for axis, count in sizes:
        for turn, met in enumerate(turns(count)):
            rows = groups[(axis, turn)]
            if len(met) == count:
                received.append(lax.ppermute(rows, axis, list(met.items())))
            else:
                received.append(lax.ppermute(rows, (axis, across), pairs_with(met, count, sides)))
    return received


def slots(sizes):
    return [(axis, turn) for axis, count in sizes for turn in range(len(turns(count)))]


def list_row(axis, x_ref, yz_ref, upper):
    if axis == "gx":
        return x_ref[upper : upper + 1, :]
    base = 0 if axis == "gy" else 2
    return yz_ref[base + upper : base + upper + 1, :]


def gather_halo(sizes, refs):
    table = []
    place = 0
    for axis, count in sizes:
        parts = []
        for _ in turns(count):
            parts.append(refs[place][...].astype(F32))
            place += 1
        table += received_slots(axis, count, parts)
    return jnp.concatenate(table, axis=0).astype(BF)


def send_kernel(sizes, x_hbm, yz_hbm, table_hbm, *rest):
    count = len(slots(sizes))
    later = (len(rest) - count - 4) // 2
    more_hbm, table_ref, outs = rest[:later], rest[later], rest[later + 1 : later + 1 + count]
    more_ref, (x_ref, yz_ref, sems) = rest[later + 1 + count : -3], rest[-3:]
    pairs = [(x_hbm, x_ref), (yz_hbm, yz_ref), (table_hbm, table_ref), *zip(more_hbm, more_ref)]
    copies = [pltpu.make_async_copy(a, b, sems.at[k]) for k, (a, b) in enumerate(pairs)]
    for copy in copies:
        copy.start()
    for copy in copies[:2]:
        copy.wait()
    nodes = table_ref.shape[0]
    picks = []
    for axis, turn in slots(sizes):
        row = send_list(
            axis, turn, list_row(axis, x_ref, yz_ref, 0), list_row(axis, x_ref, yz_ref, 1)
        )
        picks.append(hot_rows(row, nodes).astype(BF))
    copies[2].wait()
    table = table_ref[...]
    for pick, out in zip(picks, outs):
        out[...] = dot(pick, table).astype(BF)
    for copy in copies[3:]:
        copy.wait()


def own_kernel(block, latent_ref, edges_ref, from_ref, to_ref, w_ref, out_ref):
    latent = latent_ref[...]
    nodes, width = latent.shape
    half = nodes // 2
    w_edge = turned(w_ref[0, :width, :])
    from_table = halves(dot_nt(turned(w_ref[0, width : 2 * width, :]), latent).astype(BF))
    to_table = halves(dot_nt(turned(w_ref[0, 2 * width :, :]), latent).astype(BF))
    rows = block // LANES
    for step in range(edges_ref.shape[0] // block):
        senders = lane_row(from_ref, step * rows, rows)
        receivers = lane_row(to_ref, step * rows, rows)
        low = jnp.where(senders < nodes, senders & (half - 1), -1)
        got = dot_nt(w_edge, edges_ref[step * block : (step + 1) * block, :])
        got += pick_half(dot(from_table, hot(low, half)), senders >= half)
        got += pick_half(dot(to_table, hot(receivers & (half - 1), half)), receivers >= half)
        out_ref[:, step * block : (step + 1) * block] = got


def fine_kernel(
    sizes,
    csizes,
    block,
    latent_ref,
    edges_ref,
    from_ref,
    to_ref,
    cluster_ref,
    cx_ref,
    cyz_ref,
    w_in,
    w_out,
    n_in,
    n_out,
    gain_ref,
    pre_ref,
    *rest,
):
    count = len(slots(sizes))
    halo_refs, (state_ref, pooled_ref), sends = rest[:count], rest[count : count + 2], rest[count + 2 :]
    latent = latent_ref[...]
    nodes, width = latent.shape
    half = nodes // 2
    halo = gather_halo(sizes, halo_refs)
    halo_half = halo.shape[0] // 2
    halo_table = halves(dot_nt(turned(w_in[0, width : 2 * width, :]), halo).astype(BF))
    second = turned(w_out[0])
    eye = identity(width)
    gains = gain_tile(gain_ref[0, 0:1, :], block)
    rows = block // LANES
    summed = jnp.zeros((2 * width, half), F32)
    for step in range(edges_ref.shape[0] // block):
        here = slice(step * block, (step + 1) * block)
        senders = lane_row(from_ref, step * rows, rows) - nodes
        receivers = lane_row(to_ref, step * rows, rows)
        low = jnp.where(senders >= 0, senders & (halo_half - 1), -1)
        pre = pre_ref[:, here] + pick_half(dot(halo_table, hot(low, halo_half)), senders >= halo_half)
        hidden = jnp.maximum(pre, 0.0).astype(BF)
        message = dot_nt(eye, edges_ref[here, :]) + norm_columns(dot(second, hidden), gains)
        upper = receivers >= half
        both = jnp.concatenate(
            [jnp.where(upper, 0.0, message), jnp.where(upper, message, 0.0)], axis=0
        ).astype(BF)
        summed += dot_nt(both, hot(receivers & (half - 1), half))
    summed = jnp.concatenate([summed[:width], summed[width:]], axis=1).astype(BF)
    hidden = dot_nt(turned(n_in[0, :width, :]), latent) + dot(turned(n_in[0, width:, :]), summed)
    hidden = jnp.maximum(hidden, 0.0).astype(BF)
    state = dot_nt(eye, latent) + norm_columns(
        dot(turned(n_out[0]), hidden), gain_tile(gain_ref[0, 1:2, :], nodes)
    )
    state = state.astype(BF)
    state_ref[...] = state
    clusters = pooled_ref.shape[1]
    member = hot(lane_row(cluster_ref, 0, nodes // LANES), clusters)
    counts = dot_nt(jnp.ones((16, nodes), BF), member)[0:1, :]
    pooled = (dot_nt(state, member) / counts).astype(BF)
    pooled_ref[...] = pooled
    for (axis, turn), out in zip(slots(csizes), sends):
        row = send_list(
            axis, turn, list_row(axis, cx_ref, cyz_ref, 0), list_row(axis, cx_ref, cyz_ref, 1)
        )
        out[...] = dot_nt(hot_rows(row, clusters).astype(BF), pooled).astype(BF)


def coarse_own_kernel(
    halo_rows,
    state_ref,
    cluster_ref,
    pooled_ref,
    edges_ref,
    from_ref,
    to_ref,
    w_in,
    w_out,
    n_in,
    n_out,
    gain_ref,
    pre_ref,
    edges_out,
    from_out,
    to_out,
    node_ref,
    turned_ref,
    gains_ref,
    flat_ref,
    member_ref,
):
    pooled = pooled_ref[...]
    width, clusters = pooled.shape
    edges = edges_ref.shape[0]
    rows = edges // LANES
    senders = lane_row(from_ref, 0, rows)
    receivers = lane_row(to_ref, 0, rows)
    w_from = turned(w_in[1, width : 2 * width, :])
    tables = jnp.concatenate(
        [dot(w_from, pooled).astype(BF), dot(turned(w_in[1, 2 * width :, :]), pooled).astype(BF)], axis=1
    )
    hot_to = hot(receivers, clusters)
    picks = jnp.concatenate([hot(senders, clusters), hot_to], axis=0)
    own = jnp.concatenate([turned(w_in[1, :width, :]), identity(width)], axis=0)
    own = dot_nt(own, edges_ref[...])
    pre_ref[...] = own[:width] + dot(tables, picks)
    edges_out[...] = own[width:]
    from_out[...] = hot(senders - clusters, halo_rows)
    to_out[...] = hot_to
    node_ref[...] = dot(turned(n_in[1, :width, :]), pooled)
    for k, weights in enumerate((w_from, turned(w_out[1]), turned(n_in[1, width:, :]), turned(n_out[1]))):
        turned_ref[k] = weights
    for k in range(2):
        gains_ref[k] = gain_tile(gain_ref[1, k : k + 1, :], LANES)
    flat_ref[...] = state_ref[...].astype(F32).T.astype(BF)
    for k in range(cluster_ref.shape[0]):
        member_ref[k * LANES : (k + 1) * LANES, :] = hot_rows(cluster_ref[k : k + 1, :], clusters).astype(BF)


def coarse_kernel(
    sizes,
    pooled_ref,
    unpool_ref,
    pre_ref,
    edges_ref,
    from_ref,
    to_ref,
    node_ref,
    turned_ref,
    gains_ref,
    flat_ref,
    member_ref,
    *rest,
):
    halo_refs, (out_hbm, out_ref, sems) = rest[:-3], rest[-3:]
    edges = edges_ref.shape[1]
    halo = gather_halo(sizes, halo_refs)
    halo_table = dot_nt(turned_ref[0], halo).astype(BF)
    pre = pre_ref[...] + dot(halo_table, from_ref[...])
    hidden = jnp.maximum(pre, 0.0).astype(BF)
    gains = jnp.concatenate([gains_ref[0]] * (edges // LANES), axis=1)
    message = edges_ref[...] + norm_columns(dot(turned_ref[1], hidden), gains)
    summed = dot_nt(message.astype(BF), to_ref[...]).astype(BF)
    hidden = jnp.maximum(node_ref[...] + dot(turned_ref[2], summed), 0.0).astype(BF)
    state = pooled_ref[...].astype(F32) + norm_columns(dot(turned_ref[3], hidden), gains_ref[1])
    lifted = dot(state.astype(BF).astype(F32).T.astype(BF), unpool_ref[...])
    high = lifted.astype(BF)
    low = (lifted - high.astype(F32)).astype(BF)
    both = jnp.concatenate([high, low], axis=0)
    step = out_ref.shape[0] // 4
    copies = []
    for k in range(4):
        here = slice(k * step, (k + 1) * step)
        member = member_ref[here, :]
        added = dot(jnp.concatenate([member, member], axis=1), both)
        out_ref[here, :] = (flat_ref[here, :].astype(F32) + added).astype(BF)
        copies.append(pltpu.make_async_copy(out_ref.at[here], out_hbm.at[here], sems.at[k]))
        copies[-1].start()
    for copy in copies:
        copy.wait()


def call(kernel, outs, *args, space=VMEM, into=VMEM, scratch=(), flops=0, moved=0):
    single = not isinstance(outs, (list, tuple))
    shapes = [outs] if single else list(outs)
    got = pl.pallas_call(
        kernel,
        out_shape=shapes,
        in_specs=[space] * len(args),
        out_specs=[into] * len(shapes),
        scratch_shapes=list(scratch),
        cost_estimate=pl.CostEstimate(flops=flops, bytes_accessed=moved, transcendentals=0),
        compiler_params=pltpu.CompilerParams(vmem_limit_bytes=24 << 20),
    )(*args)
    return got[0] if single else got


def local(
    sizes,
    fine_latent,
    fine_edges,
    fine_from,
    fine_to,
    fine_send_x,
    fine_send_yz,
    cluster,
    coarse_edges,
    coarse_from,
    coarse_to,
    coarse_send_x,
    coarse_send_yz,
    edge_in,
    edge_out,
    node_in,
    node_out,
    norm_gain,
    unpool_weight,
):
    nodes, width = fine_latent.shape
    edges = fine_edges.shape[0]
    coarse_nodes = 128
    shape = jax.ShapeDtypeStruct

    def lanes(values):
        return values.reshape(-1, LANES)

    def send_shapes(x_list, yz_list):
        return [
            shape((x_list.shape[1] if axis == "gx" else yz_list.shape[1], width), BF)
            for axis, _ in slots(sizes)
        ]

    fine_from, fine_to, cluster = lanes(fine_from), lanes(fine_to), lanes(cluster)
    coarse_from, coarse_to = lanes(coarse_from), lanes(coarse_to)

    early = (fine_edges, fine_from, fine_to, edge_in)
    first = (fine_send_x, fine_send_yz, fine_latent, *early)
    fine_latent, *got = call(
        functools.partial(send_kernel, sizes),
        [pltpu.VMEM(fine_latent.shape, BF)]
        + send_shapes(fine_send_x, fine_send_yz)
        + [pltpu.VMEM(value.shape, value.dtype) for value in early],
        *[pltpu.with_memory_space_constraint(value, pltpu.HBM) for value in first],
        space=pl.BlockSpec(memory_space=pltpu.HBM),
        scratch=[
            pltpu.VMEM(fine_send_x.shape, jnp.int32),
            pltpu.VMEM(fine_send_yz.shape, jnp.int32),
            pltpu.SemaphoreType.DMA((len(first),)),
        ],
        flops=2_000_000_000,
        moved=1 << 20,
    )
    sends, (fine_edges, fine_from, fine_to, edge_in) = got[: -len(early)], got[-len(early) :]
    halo = exchange(dict(zip(slots(sizes), sends)), sizes)
    pre = call(
        functools.partial(own_kernel, 1024),
        shape((width, edges), F32),
        fine_latent,
        fine_edges,
        fine_from,
        fine_to,
        edge_in,
        flops=4_000_000_000,
        moved=1 << 20,
    )
    state, pooled, *sends = call(
        functools.partial(fine_kernel, sizes, sizes, 4096),
        [shape((width, nodes), BF), shape((width, coarse_nodes), BF)]
        + send_shapes(coarse_send_x, coarse_send_yz),
        fine_latent,
        fine_edges,
        fine_from,
        fine_to,
        cluster,
        coarse_send_x,
        coarse_send_yz,
        edge_in,
        edge_out,
        node_in,
        node_out,
        norm_gain,
        pre,
        *halo,
        flops=4_000_000_000,
        moved=1 << 20,
    )
    halo = exchange(dict(zip(slots(sizes), sends)), sizes)
    coarse_count = coarse_edges.shape[0]
    halo_rows = 2 * coarse_send_x.shape[1] + coarse_send_yz.size
    ready = call(
        functools.partial(coarse_own_kernel, halo_rows),
        [
            shape((width, coarse_count), F32),
            shape((width, coarse_count), F32),
            shape((halo_rows, coarse_count), BF),
            shape((coarse_nodes, coarse_count), BF),
            shape((width, coarse_nodes), F32),
            shape((4, width, width), BF),
            shape((2, width, LANES), F32),
            shape((nodes, width), BF),
            shape((nodes, coarse_nodes), BF),
        ],
        state,
        cluster,
        pooled,
        coarse_edges,
        coarse_from,
        coarse_to,
        edge_in,
        edge_out,
        node_in,
        node_out,
        norm_gain,
        flops=1_000_000_000,
        moved=1 << 20,
    )
    return call(
        functools.partial(coarse_kernel, sizes),
        shape((nodes, width), BF),
        pooled,
        unpool_weight,
        *ready,
        *halo,
        into=pl.BlockSpec(memory_space=pltpu.HBM),
        scratch=[pltpu.VMEM((nodes, width), BF), pltpu.SemaphoreType.DMA((4,))],
    )


def solution(mesh):
    sizes = tuple((axis, mesh.shape[axis]) for axis in ("gx", "gy", "gz"))
    rows = P(("grp", "gx", "gy", "gz"), None)
    flat = P(("grp", "gx", "gy", "gz"))
    in_specs = (rows, rows, flat, flat, rows, rows, flat, rows, flat, flat, rows, rows) + (P(),) * 6
    return jax.shard_map(
        functools.partial(local, sizes),
        mesh=mesh,
        in_specs=in_specs,
        out_specs=rows,
        check_vma=False,
    )
```
